32 devices in a mesh: row: 8 (over z, x), col: 4 (over y, core).
Axes of the slice: x: 2, y: 2, z: 4, core: 2. Of those that a mesh axis runs over, the one named last changes fastest.
Arguments:
- signal: bfloat16 [16384, 2048], P('row', 'col'), may hold values from -40 to 40
- norm_gain: float32 [2048], replicated, may hold values from 0.5 to 2
- qkv_weight: bfloat16 [2048, 6144], P('row', 'col'), may hold values from -4 to 4
- out_weight: bfloat16 [2048, 2048], P('row', 'col'), may hold values from -1 to 1
Outputs:
- layer_out: bfloat16 [16384, 2048], P('row', 'col')
The draws below stay inside these ranges and needn't reach their ends.
All inputs are finite; a program needn't handle non-finite values.
Results may differ from the reference program's by a relative error of at most 0.006.
Values may be sent and summed in bfloat16 or wider, within the bound.
A program may use at most 64 MiB of HBM per device.

```python
import math
import jax
import jax.numpy as jnp
from jax import lax

D = 2048
H = 16
HS = 128
COLS = 1024
ROWS = 16
TOKENS = 16384


def draw_signal(key, part):
    first_key, second_key, third_key = jax.random.split(key, 3)
    position = jnp.arange(D, dtype=jnp.float32) / (D - 1)
    feature = jnp.exp(position * math.log(3.0)) * jax.random.uniform(second_key, (D,), jnp.float32, 0.7, 1.0)
    entries = jnp.clip(jax.random.normal(first_key, (TOKENS, D), jnp.float32), -4.0, 4.0)
    row_scale = jnp.exp(jax.random.uniform(third_key, (TOKENS, 1), jnp.float32, math.log(0.3), math.log(3.0)))
    return (entries * row_scale * feature).astype(jnp.bfloat16)


def draw_qkv_weight(key, part):
    first_key = jax.random.fold_in(key, 0)
    entries = jnp.clip(jax.random.normal(first_key, (D, H, 3, HS), jnp.float32), -4.0, 4.0) / math.sqrt(D)
    return entries.reshape(D, 3 * D).astype(jnp.bfloat16)


def steps_of(key, dims, cuts, smallest, high):
    def one(axis_at, blocks):
        steps = jax.random.uniform(jax.random.fold_in(jax.random.fold_in(key, 6), axis_at), (blocks,), jnp.float32, smallest / len(cuts), high / len(cuts))
        return jnp.repeat(jnp.exp(steps), dims[axis_at] // blocks).reshape((-1,) + (1,) * (len(dims) - axis_at - 1))

    factor_of = one(*cuts[0])
    for cut in cuts[1:]:
        factor_of = factor_of * one(*cut)
    return factor_of


def centred(rng, dims, spread, most, pieces=(), held_as=jnp.bfloat16):
    result = spread * jax.random.normal(rng, dims, jnp.float32)
    if pieces:
        result = result * steps_of(rng, dims, pieces, -0.22, 0.18)
    return jnp.clip(result, -most, most).astype(held_as)


def setup_inputs(seed: int = 0) -> dict:
    seeds = jax.random.split(jax.random.key(seed), 5)
    return {
        "signal": draw_signal(jax.random.fold_in(seeds[4], 71), 0),
        "norm_gain": jnp.clip(jnp.exp(jax.random.uniform(seeds[1], (D,), jnp.float32, math.log(0.5), math.log(2.0))), 0.5, 2.0),
        "qkv_weight": draw_qkv_weight(jax.random.fold_in(seeds[4], 71), 0),
        "out_weight": centred(seeds[3], (D, D), (D // 64) ** -0.5, 1.0, ((0, 8), (1, 4))),
    }


EPSILON = 1e-05
NEGATIVE = -1e+30

def reference(signal, norm_gain, qkv_weight, out_weight):
    widened = signal.astype(jnp.float32)
    average = lax.optimization_barrier(jnp.mean(widened, axis=1, keepdims=True))
    variance = lax.optimization_barrier(jnp.mean((widened - average) ** 2, axis=1, keepdims=True))
    normed = ((widened - average) * lax.rsqrt(variance + EPSILON) * norm_gain).astype(jnp.bfloat16)
    qkv = jnp.dot(normed, qkv_weight, preferred_element_type=jnp.float32).astype(jnp.bfloat16)
    qkv = qkv.reshape(ROWS, COLS, H, 3, HS)
    factor = 1.0 / math.sqrt(HS)

    def row_softmax(row_block):
        queries = row_block[:, :, 0].astype(jnp.float32)
        key_part = row_block[:, :, 1].astype(jnp.float32)
        values = row_block[:, :, 2].astype(jnp.float32)
        scores = jnp.einsum('chd,ehd->hce', queries, key_part) * factor
        causal = jnp.arange(COLS)[:, None] >= jnp.arange(COLS)[None, :]
        scores = jnp.where(causal, scores, NEGATIVE)
        maxima = lax.optimization_barrier(jnp.max(scores, axis=-1))
        weights = jnp.where(causal, jnp.exp(scores - maxima[..., None]), 0.0)
        totals = lax.optimization_barrier(jnp.sum(weights, axis=-1))
        rounded = lax.optimization_barrier(weights.astype(jnp.bfloat16)).astype(jnp.float32)
        summed = jnp.einsum('hce,ehd->chd', rounded, values)
        return (summed, maxima.T, totals.T)
    row_acc, row_max, row_total = lax.map(row_softmax, qkv)
    queries = qkv[:, :, :, 0].astype(jnp.float32)
    key_part = qkv[:, :, :, 1].astype(jnp.float32)
    values = qkv[:, :, :, 2].astype(jnp.float32)
    scores = jnp.einsum('rchd,schd->chrs', queries, key_part) * factor
    earlier = jnp.arange(ROWS)[:, None] > jnp.arange(ROWS)[None, :]
    scores = jnp.where(earlier, scores, NEGATIVE)
    maxima = lax.optimization_barrier(jnp.max(scores, axis=-1))
    weights = jnp.where(earlier, jnp.exp(scores - maxima[..., None]), 0.0)
    totals = lax.optimization_barrier(jnp.sum(weights, axis=-1))
    rounded = lax.optimization_barrier(weights.astype(jnp.bfloat16)).astype(jnp.float32)
    col_acc = jnp.einsum('chrs,schd->rchd', rounded, values)
    col_max = jnp.transpose(maxima, (2, 0, 1))
    col_total = jnp.transpose(totals, (2, 0, 1))
    highest = jnp.maximum(row_max, col_max)
    row_factor = jnp.exp(row_max - highest)
    col_factor = jnp.exp(col_max - highest)
    denominator = row_factor * row_total + col_factor * col_total
    merged = (row_factor[..., None] * row_acc + col_factor[..., None] * col_acc) / denominator[..., None]
    attended = merged.astype(jnp.bfloat16).reshape(ROWS * COLS, H * HS)
    branch = jnp.dot(attended, out_weight, preferred_element_type=jnp.float32)
    return (widened + branch).astype(jnp.bfloat16)
```

```python
import functools
import math

import jax
import jax.numpy as jnp
from jax import lax
from jax.experimental import pallas as pl
from jax.experimental.pallas import tpu as pltpu
from jax.sharding import PartitionSpec as P

HS = 128
COLS = 1024
GROUP = 16
LANES = 128

EPSILON = 1e-05
NEGATIVE = -1e30
VMEM_LIMIT = 56 * 1024 * 1024
F32 = jnp.float32
BF16 = jnp.bfloat16


def block_of(size, most):
    while size % most:
        most //= 2
    return most


def norm_project_kernel(sig_ref, gain_ref, weight_ref, out_ref):
    pieces, _, width = sig_ref.shape
    parts = [sig_ref[i].astype(F32) for i in range(pieces)]
    total = sum(jnp.sum(part, axis=1, keepdims=True) for part in parts)
    average = total / (pieces * width)
    parts = [part - average for part in parts]
    squares = sum(jnp.sum(part * part, axis=1, keepdims=True) for part in parts)
    scale = lax.rsqrt(squares / (pieces * width) + EPSILON)
    normed = jnp.concatenate(
        [
            (part * scale * gain_ref[:, i * width : (i + 1) * width]).astype(BF16)
            for i, part in enumerate(parts)
        ],
        axis=1,
    )
    out_ref[...] = jnp.dot(normed, weight_ref[...], preferred_element_type=F32).astype(BF16)


def norm_project(gathered, norm_gain, weight):
    pieces, tokens, width = gathered.shape
    features, outs = weight.shape
    block = block_of(tokens, 256)
    return pl.pallas_call(
        norm_project_kernel,
        out_shape=jax.ShapeDtypeStruct((tokens, outs), BF16),
        grid=(tokens // block,),
        in_specs=[
            pl.BlockSpec((pieces, block, width), lambda i: (0, i, 0)),
            pl.BlockSpec((1, features), lambda i: (0, 0)),
            pl.BlockSpec((features, outs), lambda i: (0, 0)),
        ],
        out_specs=pl.BlockSpec((block, outs), lambda i: (i, 0)),
        compiler_params=pltpu.CompilerParams(vmem_limit_bytes=VMEM_LIMIT),
        cost_estimate=pl.CostEstimate(
            flops=2 * tokens * features * outs,
            bytes_accessed=2 * (tokens * features + features * outs + tokens * outs),
            transcendentals=0,
        ),
    )(gathered, norm_gain.reshape(1, features), weight)


def softmax_part(queries, keys, values, allowed):
    factor = 1.0 / math.sqrt(HS)
    scores = lax.dot_general(
        queries, keys, (((1,), (1,)), ((), ())), preferred_element_type=F32
    )
    if allowed is not None:
        first = scores.shape[1] - allowed.shape[1]
        tail = jnp.where(allowed, scores[:, first:], NEGATIVE)
        scores = tail if first == 0 else jnp.concatenate([scores[:, :first], tail], axis=1)
    top = jnp.max(scores, axis=1, keepdims=True)
    weights = jnp.exp2((scores - top) * (factor * math.log2(math.e)))
    return scores, top, weights, factor


def row_kernel(qkv_ref, acc_ref, stat_ref, *, heads, block):
    length = qkv_ref.shape[0]
    line = lax.broadcasted_iota(jnp.int32, (block, block), 0)
    lane = lax.broadcasted_iota(jnp.int32, (block, block), 1)
    allowed = line >= lane
    place = lax.broadcasted_iota(jnp.int32, (block, LANES), 1)
    for part in range(length // block):
        rows = slice(part * block, (part + 1) * block)
        reach = slice(0, (part + 1) * block)
        stats = jnp.zeros((block, LANES), F32)
        for head in range(heads):
            at = head * 3 * HS
            _, top, weights, factor = softmax_part(
                qkv_ref[rows, at : at + HS],
                qkv_ref[reach, at + HS : at + 2 * HS],
                None,
                allowed,
            )
            total = jnp.sum(weights, axis=1, keepdims=True)
            summed = jnp.dot(
                weights.astype(BF16),
                qkv_ref[reach, at + 2 * HS : at + 3 * HS],
                preferred_element_type=F32,
            )
            acc_ref[rows, head * HS : (head + 1) * HS] = summed
            stats = jnp.where(place == head, top * factor, stats)
            stats = jnp.where(place == heads + head, total, stats)
        stat_ref[rows, :] = stats


def row_attention(qkv, heads):
    tokens, width = qkv.shape
    return pl.pallas_call(
        functools.partial(row_kernel, heads=heads, block=block_of(COLS, 256)),
        out_shape=(
            jax.ShapeDtypeStruct((tokens, heads * HS), F32),
            jax.ShapeDtypeStruct((tokens, LANES), F32),
        ),
        grid=(tokens // COLS,),
        in_specs=[pl.BlockSpec((COLS, width), lambda i: (i, 0))],
        out_specs=(
            pl.BlockSpec((COLS, heads * HS), lambda i: (i, 0)),
            pl.BlockSpec((COLS, LANES), lambda i: (i, 0)),
        ),
        compiler_params=pltpu.CompilerParams(vmem_limit_bytes=VMEM_LIMIT),
        cost_estimate=pl.CostEstimate(
            flops=4 * tokens * COLS * heads * HS,
            bytes_accessed=2 * tokens * width + 4 * tokens * heads * HS,
            transcendentals=tokens * COLS * heads,
        ),
    )(qkv)


def column_kernel(qkv_ref, mean_ref, stat_ref, *, heads):
    lines = qkv_ref.shape[0]
    count = lines * GROUP
    line = lax.broadcasted_iota(jnp.int32, (count, count), 0)
    lane = lax.broadcasted_iota(jnp.int32, (count, count), 1)
    allowed = jnp.logical_and(
        lax.rem(line, GROUP) == lax.rem(lane, GROUP), line // GROUP > lane // GROUP
    )
    place = lax.broadcasted_iota(jnp.int32, (count, LANES), 1)
    some = lax.broadcasted_iota(jnp.int32, (count, 1), 0) >= GROUP
    stats = jnp.zeros((count, LANES), F32)
    for head in range(heads):
        at = head * 3 * HS
        queries, keys, values = (
            qkv_ref[:, :, at + i * HS : at + (i + 1) * HS].reshape(count, HS) for i in range(3)
        )
        _, top, weights, factor = softmax_part(queries, keys, None, allowed)
        weights = jnp.where(allowed, weights, 0.0)
        total = jnp.sum(weights, axis=1, keepdims=True)
        summed = jnp.dot(weights.astype(BF16), values, preferred_element_type=F32)
        mean = jnp.where(some, summed / jnp.where(some, total, 1.0), 0.0)
        mean_ref[:, :, head * HS : (head + 1) * HS] = mean.astype(BF16).reshape(
            lines, GROUP, HS
        )
        stats = jnp.where(place == head, jnp.where(some, top * factor, NEGATIVE), stats)
        stats = jnp.where(place == heads + head, total, stats)
    stat_ref[0] = stats.T[: stat_ref.shape[1], :]


def column_attention(qkv, heads, held):
    lines, columns, width = qkv.shape
    groups = columns // GROUP
    return pl.pallas_call(
        functools.partial(column_kernel, heads=heads),
        out_shape=(
            jax.ShapeDtypeStruct((lines, columns, heads * HS), BF16),
            jax.ShapeDtypeStruct((groups, held, lines * GROUP), F32),
        ),
        grid=(groups,),
        in_specs=[pl.BlockSpec((lines, GROUP, width), lambda i: (0, i, 0))],
        out_specs=(
            pl.BlockSpec((lines, GROUP, heads * HS), lambda i: (0, i, 0)),
            pl.BlockSpec((1, held, lines * GROUP), lambda i: (i, 0, 0)),
        ),
        compiler_params=pltpu.CompilerParams(vmem_limit_bytes=VMEM_LIMIT),
    )(qkv)


def merge_kernel(acc_ref, rstat_ref, mean_ref, cstat_ref, out_ref, *, heads):
    rstat = rstat_ref[...]
    held, block = cstat_ref.shape[1:]
    cstat = cstat_ref[0]
    if held < LANES:
        cstat = jnp.concatenate([cstat, jnp.zeros((LANES - held, block), F32)], axis=0)
    cstat = cstat.T
    sources, _, columns, _ = mean_ref.shape
    for head in range(heads):
        across = slice(head * HS, (head + 1) * HS)
        row_max = rstat[:, head : head + 1]
        row_total = rstat[:, heads + head : heads + head + 1]
        col_max = cstat[:, head : head + 1]
        col_total = cstat[:, heads + head : heads + head + 1]
        top = jnp.maximum(row_max, col_max)
        row_factor = jnp.exp(row_max - top)
        col_part = jnp.exp(col_max - top) * col_total
        share = 1.0 / (row_factor * row_total + col_part)
        mean = mean_ref[:, 0, :, across].reshape(sources * columns, HS).astype(F32)
        out_ref[:, across] = (
            (row_factor * share) * acc_ref[:, across] + (col_part * share) * mean
        ).astype(BF16)


def merge(row_acc, row_stats, col_mean, col_stats, heads):
    tokens, width = row_acc.shape
    sources, _, columns, _ = col_mean.shape
    held = col_stats.shape[1]
    return pl.pallas_call(
        functools.partial(merge_kernel, heads=heads),
        out_shape=jax.ShapeDtypeStruct((tokens, width), BF16),
        grid=(tokens // COLS,),
        in_specs=[
            pl.BlockSpec((COLS, width), lambda i: (i, 0)),
            pl.BlockSpec((COLS, LANES), lambda i: (i, 0)),
            pl.BlockSpec((sources, 1, columns, width), lambda i: (0, i, 0, 0)),
            pl.BlockSpec((1, held, COLS), lambda i: (i, 0, 0)),
        ],
        out_specs=pl.BlockSpec((COLS, width), lambda i: (i, 0)),
        compiler_params=pltpu.CompilerParams(vmem_limit_bytes=VMEM_LIMIT),
    )(row_acc, row_stats, col_mean, col_stats)


def project_kernel(att_ref, weight_ref, signal_ref, out_ref):
    pieces, _, width = att_ref.shape
    joined = jnp.concatenate([att_ref[i] for i in range(pieces)], axis=1)
    branch = jnp.dot(joined, weight_ref[...], preferred_element_type=F32)
    out_ref[...] = (signal_ref[...].astype(F32) + branch).astype(BF16)


def project(gathered, weight, signal):
    pieces, tokens, width = gathered.shape
    features, outs = weight.shape
    block = block_of(tokens, 256)
    return pl.pallas_call(
        project_kernel,
        out_shape=jax.ShapeDtypeStruct((tokens, outs), BF16),
        grid=(tokens // block,),
        in_specs=[
            pl.BlockSpec((pieces, block, width), lambda i: (0, i, 0)),
            pl.BlockSpec((features, outs), lambda i: (0, 0)),
            pl.BlockSpec((block, outs), lambda i: (i, 0)),
        ],
        out_specs=pl.BlockSpec((block, outs), lambda i: (i, 0)),
        compiler_params=pltpu.CompilerParams(vmem_limit_bytes=VMEM_LIMIT),
    )(gathered, weight, signal)


def per_device(signal, norm_gain, qkv_weight, out_weight):
    samples, width = signal.shape
    count = lax.axis_size("row")
    rows_here = samples // COLS
    lines = rows_here * count
    columns = COLS // count
    heads = qkv_weight.shape[1] // (3 * HS)
    held = -(-2 * heads // 8) * 8

    spread = jnp.transpose(signal.reshape(rows_here, count, columns, width), (1, 0, 2, 3))
    crossed = lax.all_to_all(spread, "row", split_axis=0, concat_axis=0, tiled=True)
    crossed = crossed.reshape(lines * columns, width)
    piece_qkv = lax.all_gather(qkv_weight, "row", axis=0, tiled=True)
    col_signal = lax.all_gather(crossed, "col", axis=0)
    row_signal = lax.all_gather(signal, "col", axis=0)
    piece_out = lax.all_gather(out_weight, "row", axis=0, tiled=True)

    col_qkv = norm_project(col_signal, norm_gain, piece_qkv)
    col_mean, col_stats = column_attention(
        col_qkv.reshape(lines, columns, 3 * heads * HS), heads, held
    )
    col_stats = jnp.transpose(
        col_stats.reshape(columns // GROUP, held, lines, GROUP), (2, 1, 0, 3)
    ).reshape(lines, held, columns)
    col_stats = lax.all_to_all(col_stats, "row", split_axis=0, concat_axis=2, tiled=True)
    col_mean = lax.all_to_all(
        col_mean.reshape(count, rows_here, columns, heads * HS),
        "row",
        split_axis=0,
        concat_axis=0,
        tiled=True,
    )
    row_qkv = norm_project(row_signal, norm_gain, piece_qkv)
    row_acc, row_stats = row_attention(row_qkv, heads)
    attended = merge(row_acc, row_stats, col_mean, col_stats, heads)
    return project(lax.all_gather(attended, "col", axis=0), piece_out, signal)


def solution(mesh):
    return jax.shard_map(
        per_device,
        mesh=mesh,
        in_specs=(P("row", "col"), P(), P("row", "col"), P("row", "col")),
        out_specs=P("row", "col"),
        check_vma=False,
    )
```

```python
import functools
import math

import jax
import jax.numpy as jnp
from jax import lax
from jax.experimental import pallas as pl
from jax.experimental.pallas import tpu as pltpu
from jax.sharding import PartitionSpec as P

HS = 128
COLS = 1024
GROUP = 16
LANES = 128

EPSILON = 1e-05
NEGATIVE = -1e30
VMEM_LIMIT = 56 * 1024 * 1024
F32 = jnp.float32
BF16 = jnp.bfloat16


def block_of(size, most):
    while size % most:
        most //= 2
    return most


def norm_project_kernel(sig_ref, gain_ref, weight_ref, out_ref):
    pieces, _, width = sig_ref.shape
    parts = [sig_ref[i].astype(F32) for i in range(pieces)]
    total = sum(jnp.sum(part, axis=1, keepdims=True) for part in parts)
    average = total / (pieces * width)
    parts = [part - average for part in parts]
    squares = sum(jnp.sum(part * part, axis=1, keepdims=True) for part in parts)
    scale = lax.rsqrt(squares / (pieces * width) + EPSILON)
    normed = jnp.concatenate(
        [
            (part * scale * gain_ref[:, i * width : (i + 1) * width]).astype(BF16)
            for i, part in enumerate(parts)
        ],
        axis=1,
    )
    out_ref[...] = jnp.dot(normed, weight_ref[...], preferred_element_type=F32).astype(BF16)


def norm_project(gathered, norm_gain, weight):
    pieces, tokens, width = gathered.shape
    features, outs = weight.shape
    block = block_of(tokens, 256)
    return pl.pallas_call(
        norm_project_kernel,
        out_shape=jax.ShapeDtypeStruct((tokens, outs), BF16),
        grid=(tokens // block,),
        in_specs=[
            pl.BlockSpec((pieces, block, width), lambda i: (0, i, 0)),
            pl.BlockSpec((1, features), lambda i: (0, 0)),
            pl.BlockSpec((features, outs), lambda i: (0, 0)),
        ],
        out_specs=pl.BlockSpec((block, outs), lambda i: (i, 0)),
        compiler_params=pltpu.CompilerParams(vmem_limit_bytes=VMEM_LIMIT),
        cost_estimate=pl.CostEstimate(
            flops=2 * tokens * features * outs,
            bytes_accessed=2 * (tokens * features + features * outs + tokens * outs),
            transcendentals=0,
        ),
    )(gathered, norm_gain.reshape(1, features), weight)


def softmax_part(queries, keys, values, allowed):
    factor = 1.0 / math.sqrt(HS)
    scores = lax.dot_general(
        queries, keys, (((1,), (1,)), ((), ())), preferred_element_type=F32
    )
    if allowed is not None:
        first = scores.shape[1] - allowed.shape[1]
        tail = jnp.where(allowed, scores[:, first:], NEGATIVE)
        scores = tail if first == 0 else jnp.concatenate([scores[:, :first], tail], axis=1)
    top = jnp.max(scores, axis=1, keepdims=True)
    weights = jnp.exp2((scores - top) * (factor * math.log2(math.e)))
    return scores, top, weights, factor


def row_kernel(qkv_ref, acc_ref, stat_ref, *, heads, block):
    length = qkv_ref.shape[0]
    line = lax.broadcasted_iota(jnp.int32, (block, block), 0)
    lane = lax.broadcasted_iota(jnp.int32, (block, block), 1)
    allowed = line >= lane
    place = lax.broadcasted_iota(jnp.int32, (block, LANES), 1)
    for part in range(length // block):
        rows = slice(part * block, (part + 1) * block)
        reach = slice(0, (part + 1) * block)
        stats = jnp.zeros((block, LANES), F32)
        for head in range(heads):
            at = head * 3 * HS
            _, top, weights, factor = softmax_part(
                qkv_ref[rows, at : at + HS],
                qkv_ref[reach, at + HS : at + 2 * HS],
                None,
                allowed,
            )
            total = jnp.sum(weights, axis=1, keepdims=True)
            summed = jnp.dot(
                weights.astype(BF16),
                qkv_ref[reach, at + 2 * HS : at + 3 * HS],
                preferred_element_type=F32,
            )
            acc_ref[rows, head * HS : (head + 1) * HS] = summed
            stats = jnp.where(place == head, top * factor, stats)
            stats = jnp.where(place == heads + head, total, stats)
        stat_ref[rows, :] = stats


def row_attention(qkv, heads):
    tokens, width = qkv.shape
    return pl.pallas_call(
        functools.partial(row_kernel, heads=heads, block=block_of(COLS, 256)),
        out_shape=(
            jax.ShapeDtypeStruct((tokens, heads * HS), F32),
            jax.ShapeDtypeStruct((tokens, LANES), F32),
        ),
        grid=(tokens // COLS,),
        in_specs=[pl.BlockSpec((COLS, width), lambda i: (i, 0))],
        out_specs=(
            pl.BlockSpec((COLS, heads * HS), lambda i: (i, 0)),
            pl.BlockSpec((COLS, LANES), lambda i: (i, 0)),
        ),
        compiler_params=pltpu.CompilerParams(vmem_limit_bytes=VMEM_LIMIT),
        cost_estimate=pl.CostEstimate(
            flops=4 * tokens * COLS * heads * HS,
            bytes_accessed=2 * tokens * width + 4 * tokens * heads * HS,
            transcendentals=tokens * COLS * heads,
        ),
    )(qkv)


def column_kernel(qkv_ref, mean_ref, stat_ref, *, heads):
    lines = qkv_ref.shape[0]
    count = lines * GROUP
    line = lax.broadcasted_iota(jnp.int32, (count, count), 0)
    lane = lax.broadcasted_iota(jnp.int32, (count, count), 1)
    allowed = jnp.logical_and(
        lax.rem(line, GROUP) == lax.rem(lane, GROUP), line // GROUP > lane // GROUP
    )
    place = lax.broadcasted_iota(jnp.int32, (count, LANES), 1)
    some = lax.broadcasted_iota(jnp.int32, (count, 1), 0) >= GROUP
    stats = jnp.zeros((count, LANES), F32)
    for head in range(heads):
        at = head * 3 * HS
        queries, keys, values = (
            qkv_ref[:, :, at + i * HS : at + (i + 1) * HS].reshape(count, HS) for i in range(3)
        )
        _, top, weights, factor = softmax_part(queries, keys, None, allowed)
        weights = jnp.where(allowed, weights, 0.0)
        total = jnp.sum(weights, axis=1, keepdims=True)
        summed = jnp.dot(weights.astype(BF16), values, preferred_element_type=F32)
        mean = jnp.where(some, summed / jnp.where(some, total, 1.0), 0.0)
        mean_ref[:, :, head * HS : (head + 1) * HS] = mean.astype(BF16).reshape(
            lines, GROUP, HS
        )
        stats = jnp.where(place == head, jnp.where(some, top * factor, NEGATIVE), stats)
        stats = jnp.where(place == heads + head, total, stats)
    stat_ref[0] = stats.T[: stat_ref.shape[1], :]


def column_attention(qkv, heads, held):
    lines, columns, width = qkv.shape
    groups = columns // GROUP
    return pl.pallas_call(
        functools.partial(column_kernel, heads=heads),
        out_shape=(
            jax.ShapeDtypeStruct((lines, columns, heads * HS), BF16),
            jax.ShapeDtypeStruct((groups, held, lines * GROUP), F32),
        ),
        grid=(groups,),
        in_specs=[pl.BlockSpec((lines, GROUP, width), lambda i: (0, i, 0))],
        out_specs=(
            pl.BlockSpec((lines, GROUP, heads * HS), lambda i: (0, i, 0)),
            pl.BlockSpec((1, held, lines * GROUP), lambda i: (i, 0, 0)),
        ),
        compiler_params=pltpu.CompilerParams(vmem_limit_bytes=VMEM_LIMIT),
    )(qkv)


def merge_kernel(acc_ref, rstat_ref, mean_ref, cstat_ref, out_ref, *, heads):
    rstat = rstat_ref[...]
    held, block = cstat_ref.shape[1:]
    cstat = cstat_ref[0]
    if held < LANES:
        cstat = jnp.concatenate([cstat, jnp.zeros((LANES - held, block), F32)], axis=0)
    cstat = cstat.T
    sources, _, columns, _ = mean_ref.shape
    for head in range(heads):
        across = slice(head * HS, (head + 1) * HS)
        row_max = rstat[:, head : head + 1]
        row_total = rstat[:, heads + head : heads + head + 1]
        col_max = cstat[:, head : head + 1]
        col_total = cstat[:, heads + head : heads + head + 1]
        top = jnp.maximum(row_max, col_max)
        row_factor = jnp.exp(row_max - top)
        col_part = jnp.exp(col_max - top) * col_total
        share = 1.0 / (row_factor * row_total + col_part)
        mean = mean_ref[:, 0, :, across].reshape(sources * columns, HS).astype(F32)
        out_ref[:, across] = (
            (row_factor * share) * acc_ref[:, across] + (col_part * share) * mean
        ).astype(BF16)


def merge(row_acc, row_stats, col_mean, col_stats, heads):
    tokens, width = row_acc.shape
    sources, _, columns, _ = col_mean.shape
    held = col_stats.shape[1]
    return pl.pallas_call(
        functools.partial(merge_kernel, heads=heads),
        out_shape=jax.ShapeDtypeStruct((tokens, width), BF16),
        grid=(tokens // COLS,),
        in_specs=[
            pl.BlockSpec((COLS, width), lambda i: (i, 0)),
            pl.BlockSpec((COLS, LANES), lambda i: (i, 0)),
            pl.BlockSpec((sources, 1, columns, width), lambda i: (0, i, 0, 0)),
            pl.BlockSpec((1, held, COLS), lambda i: (i, 0, 0)),
        ],
        out_specs=pl.BlockSpec((COLS, width), lambda i: (i, 0)),
        compiler_params=pltpu.CompilerParams(vmem_limit_bytes=VMEM_LIMIT),
    )(row_acc, row_stats, col_mean, col_stats)


def project_kernel(att_ref, weight_ref, signal_ref, out_ref):
    pieces, _, width = att_ref.shape
    joined = jnp.concatenate([att_ref[i] for i in range(pieces)], axis=1)
    branch = jnp.dot(joined, weight_ref[...], preferred_element_type=F32)
    out_ref[...] = (signal_ref[...].astype(F32) + branch).astype(BF16)


def project(gathered, weight, signal):
    pieces, tokens, width = gathered.shape
    features, outs = weight.shape
    block = block_of(tokens, 256)
    return pl.pallas_call(
        project_kernel,
        out_shape=jax.ShapeDtypeStruct((tokens, outs), BF16),
        grid=(tokens // block,),
        in_specs=[
            pl.BlockSpec((pieces, block, width), lambda i: (0, i, 0)),
            pl.BlockSpec((features, outs), lambda i: (0, 0)),
            pl.BlockSpec((block, outs), lambda i: (i, 0)),
        ],
        out_specs=pl.BlockSpec((block, outs), lambda i: (i, 0)),
        compiler_params=pltpu.CompilerParams(vmem_limit_bytes=VMEM_LIMIT),
    )(gathered, weight, signal)


def remote(src, dst, sems, at, target):
    return pltpu.make_async_remote_copy(
        src_ref=src,
        dst_ref=dst,
        send_sem=sems[0].at[at],
        recv_sem=sems[1].at[at],
        device_id=target,
        device_id_type=pl.DeviceIdType.MESH,
    )


def ring_place(row, half):
    return (row // 2) * (1 - row % 2) + (2 * half - 1 - row // 2) * (row % 2)


def ring_row(place, half):
    over = place // half
    return 2 * place * (1 - over) + (2 * (2 * half - 1 - place) + 1) * over


def arrive_kernel(
    signal_ref,
    weight_ref,
    crossed_ref,
    whole_ref,
    cross_send,
    cross_recv,
    peer_send,
    peer_recv,
    twin_send,
    twin_recv,
    ring_send,
    ring_recv,
    local_sem,
    *,
    count,
    pieces,
):
    row, col = lax.axis_index("row"), lax.axis_index("col")
    rows_here = signal_ref.shape[0]
    depth = weight_ref.shape[0]
    half = count // 2
    chips = pieces // 2
    twin = (row, col + 1 - 2 * (col % 2))
    peers = [(row, (col + 2 * k) % pieces) for k in range(1, chips)]
    others = [((row + k) % count, col) for k in range(1, count)]

    barrier = pltpu.get_barrier_semaphore()
    for target in others + peers + [twin]:
        pl.semaphore_signal(
            barrier, inc=1, device_id=target, device_id_type=pl.DeviceIdType.MESH
        )
    pl.semaphore_wait(barrier, len(others) + len(peers) + 1)

    def chunk(source_row, source_col):
        return crossed_ref.at[source_col, pl.ds(source_row * rows_here, rows_here)]

    started = []

    def go(copy):
        copy.start()
        started.append(copy)
        return copy

    own = signal_ref.at[:, row]
    keep = pltpu.make_async_copy(own, chunk(row, col), local_sem.at[0])
    keep.start()
    place = ring_place(row, half)
    after = (ring_row((place + 1) % count, half), col)
    before = (ring_row((place + count - 1) % count, half), col)

    def shard(owner, step):
        if step < half - 1:
            return [pl.ds(owner * depth, depth)] * 2
        return [
            pl.ds(owner * depth, depth // 2),
            pl.ds(owner * depth + depth // 2, depth // 2),
        ]

    ring = []

    def ring_step(step):
        for way, target in ((0, after), (1, before)):
            offset = count - step if way == 0 else step
            owner = ring_row((place + offset) % count, half)
            where = shard(owner, step)[way]
            if step == 0:
                source = weight_ref
                if half == 1:
                    source = weight_ref.at[pl.ds(way * (depth // 2), depth // 2)]
            else:
                source = whole_ref.at[where]
            ring.append(
                go(
                    remote(
                        source,
                        whole_ref.at[where],
                        (ring_send, ring_recv),
                        2 * step + way,
                        target,
                    )
                )
            )

    def spread(at, source, source_row):
        sent = []
        for j, target in enumerate(peers):
            sent.append(
                go(
                    remote(
                        source,
                        chunk(source_row, col),
                        (peer_send, peer_recv),
                        at * (chips - 1) + j,
                        target,
                    )
                )
            )
        go(remote(source, chunk(source_row, col), (twin_send, twin_recv), at * chips, twin))
        return sent

    def pass_on(at, sent, source_row):
        for j, copy in enumerate(sent):
            copy.wait_recv()
            piece = chunk(source_row, (col + pieces - 2 * (j + 1)) % pieces)
            go(remote(piece, piece, (twin_send, twin_recv), at * chips + 1 + j, twin))

    crossing = []
    for k, target in enumerate(others):
        crossing.append(
            go(
                remote(
                    signal_ref.at[:, target[0]],
                    chunk(row, col),
                    (cross_send, cross_recv),
                    k,
                    target,
                )
            )
        )
    pending = (0, spread(0, own, row), row)
    ring_step(0)
    hold = pltpu.make_async_copy(
        weight_ref, whole_ref.at[pl.ds(row * depth, depth)], local_sem.at[1]
    )
    hold.start()
    step = 1
    for k in range(1, count):
        crossing[k - 1].wait_recv()
        source_row = (row + count - k) % count
        later = (k, spread(k, chunk(source_row, col), source_row), source_row)
        pass_on(*pending)
        pending = later
        if k % 2 == 0 and step < half:
            for copy in ring[2 * step - 2 : 2 * step]:
                copy.wait_recv()
            ring_step(step)
            step += 1
    pass_on(*pending)
    for copy in ring[2 * half - 2 :]:
        copy.wait_recv()
    for at in range(count * chips):
        remote(own, chunk(row, col), (twin_send, twin_recv), at, twin).wait_recv()
    for copy in started:
        copy.wait_send()
    keep.wait()
    hold.wait()


def arrive(signal, weight, count, pieces):
    rows_here, _, columns, width = signal.shape
    depth, outs = weight.shape
    chips = pieces // 2
    dma = pltpu.SemaphoreType.DMA
    sizes = (count - 1, max(1, count * (chips - 1)), count * chips, count)
    return pl.pallas_call(
        functools.partial(arrive_kernel, count=count, pieces=pieces),
        out_shape=(
            jax.ShapeDtypeStruct((pieces, rows_here * count, columns, width), BF16),
            jax.ShapeDtypeStruct((depth * count, outs), BF16),
        ),
        in_specs=[pl.BlockSpec(memory_space=pl.ANY)] * 2,
        out_specs=(pl.BlockSpec(memory_space=pl.ANY),) * 2,
        scratch_shapes=[dma((size,)) for size in sizes for _ in range(2)] + [dma((2,))],
        compiler_params=pltpu.CompilerParams(collective_id=0, has_side_effects=True),
        cost_estimate=pl.CostEstimate(
            flops=0, bytes_accessed=300 * 1024 * 1024, transcendentals=0
        ),
    )(signal, weight)


def per_device(signal, norm_gain, qkv_weight, out_weight):
    samples, width = signal.shape
    count = lax.axis_size("row")
    rows_here = samples // COLS
    lines = rows_here * count
    columns = COLS // count
    heads = qkv_weight.shape[1] // (3 * HS)
    held = -(-2 * heads // 8) * 8

    pieces = lax.axis_size("col")
    col_signal, piece_qkv = arrive(
        signal.reshape(rows_here, count, columns, width), qkv_weight, count, pieces
    )
    col_signal = col_signal.reshape(pieces, lines * columns, width)
    row_signal = lax.all_gather(signal, "col", axis=0)
    piece_out = lax.all_gather(out_weight, "row", axis=0, tiled=True)

    col_qkv = norm_project(col_signal, norm_gain, piece_qkv)
    col_mean, col_stats = column_attention(
        col_qkv.reshape(lines, columns, 3 * heads * HS), heads, held
    )
    col_stats = jnp.transpose(
        col_stats.reshape(columns // GROUP, held, lines, GROUP), (2, 1, 0, 3)
    ).reshape(lines, held, columns)
    col_stats = lax.all_to_all(col_stats, "row", split_axis=0, concat_axis=2, tiled=True)
    col_mean = lax.all_to_all(
        col_mean.reshape(count, rows_here, columns, heads * HS),
        "row",
        split_axis=0,
        concat_axis=0,
        tiled=True,
    )
    row_qkv = norm_project(row_signal, norm_gain, piece_qkv)
    row_acc, row_stats = row_attention(row_qkv, heads)
    attended = merge(row_acc, row_stats, col_mean, col_stats, heads)
    return project(lax.all_gather(attended, "col", axis=0), piece_out, signal)


def solution(mesh):
    return jax.shard_map(
        per_device,
        mesh=mesh,
        in_specs=(P("row", "col"), P(), P("row", "col"), P("row", "col")),
        out_specs=P("row", "col"),
        check_vma=False,
    )
```

```python
import functools
import math

import jax
import jax.numpy as jnp
from jax import lax
from jax.experimental import pallas as pl
from jax.experimental.pallas import tpu as pltpu
from jax.sharding import PartitionSpec as P

HS = 128
COLS = 1024
GROUP = 16
LANES = 128

EPSILON = 1e-05
NEGATIVE = -1e30
VMEM_LIMIT = 56 * 1024 * 1024
F32 = jnp.float32
BF16 = jnp.bfloat16


def block_of(size, most):
    while size % most:
        most //= 2
    return most


def norm_project_kernel(sig_ref, gain_ref, weight_ref, out_ref):
    pieces, _, width = sig_ref.shape
    parts = [sig_ref[i].astype(F32) for i in range(pieces)]
    total = sum(jnp.sum(part, axis=1, keepdims=True) for part in parts)
    average = total / (pieces * width)
    parts = [part - average for part in parts]
    squares = sum(jnp.sum(part * part, axis=1, keepdims=True) for part in parts)
    scale = lax.rsqrt(squares / (pieces * width) + EPSILON)
    normed = jnp.concatenate(
        [
            (part * scale * gain_ref[:, i * width : (i + 1) * width]).astype(BF16)
            for i, part in enumerate(parts)
        ],
        axis=1,
    )
    out_ref[...] = jnp.dot(normed, weight_ref[...], preferred_element_type=F32).astype(BF16)


def norm_project(gathered, norm_gain, weight):
    pieces, tokens, width = gathered.shape
    features, outs = weight.shape
    block = block_of(tokens, 256)
    return pl.pallas_call(
        norm_project_kernel,
        out_shape=jax.ShapeDtypeStruct((tokens, outs), BF16),
        grid=(tokens // block,),
        in_specs=[
            pl.BlockSpec((pieces, block, width), lambda i: (0, i, 0)),
            pl.BlockSpec((1, features), lambda i: (0, 0)),
            pl.BlockSpec((features, outs), lambda i: (0, 0)),
        ],
        out_specs=pl.BlockSpec((block, outs), lambda i: (i, 0)),
        compiler_params=pltpu.CompilerParams(vmem_limit_bytes=VMEM_LIMIT),
        cost_estimate=pl.CostEstimate(
            flops=2 * tokens * features * outs,
            bytes_accessed=2 * (tokens * features + features * outs + tokens * outs),
            transcendentals=0,
        ),
    )(gathered, norm_gain.reshape(1, features), weight)


def softmax_part(queries, keys, values, allowed):
    factor = 1.0 / math.sqrt(HS)
    scores = lax.dot_general(
        queries, keys, (((1,), (1,)), ((), ())), preferred_element_type=F32
    )
    if allowed is not None:
        first = scores.shape[1] - allowed.shape[1]
        tail = jnp.where(allowed, scores[:, first:], NEGATIVE)
        scores = tail if first == 0 else jnp.concatenate([scores[:, :first], tail], axis=1)
    top = jnp.max(scores, axis=1, keepdims=True)
    weights = jnp.exp2((scores - top) * (factor * math.log2(math.e)))
    return scores, top, weights, factor


def row_kernel(qkv_ref, acc_ref, stat_ref, *, heads, block):
    length = qkv_ref.shape[0]
    line = lax.broadcasted_iota(jnp.int32, (block, block), 0)
    lane = lax.broadcasted_iota(jnp.int32, (block, block), 1)
    allowed = line >= lane
    place = lax.broadcasted_iota(jnp.int32, (block, LANES), 1)
    for part in range(length // block):
        rows = slice(part * block, (part + 1) * block)
        reach = slice(0, (part + 1) * block)
        stats = jnp.zeros((block, LANES), F32)
        for head in range(heads):
            at = head * 3 * HS
            _, top, weights, factor = softmax_part(
                qkv_ref[rows, at : at + HS],
                qkv_ref[reach, at + HS : at + 2 * HS],
                None,
                allowed,
            )
            total = jnp.sum(weights, axis=1, keepdims=True)
            summed = jnp.dot(
                weights.astype(BF16),
                qkv_ref[reach, at + 2 * HS : at + 3 * HS],
                preferred_element_type=F32,
            )
            acc_ref[rows, head * HS : (head + 1) * HS] = summed
            stats = jnp.where(place == head, top * factor, stats)
            stats = jnp.where(place == heads + head, total, stats)
        stat_ref[rows, :] = stats


def row_attention(qkv, heads):
    tokens, width = qkv.shape
    return pl.pallas_call(
        functools.partial(row_kernel, heads=heads, block=block_of(COLS, 256)),
        out_shape=(
            jax.ShapeDtypeStruct((tokens, heads * HS), F32),
            jax.ShapeDtypeStruct((tokens, LANES), F32),
        ),
        grid=(tokens // COLS,),
        in_specs=[pl.BlockSpec((COLS, width), lambda i: (i, 0))],
        out_specs=(
            pl.BlockSpec((COLS, heads * HS), lambda i: (i, 0)),
            pl.BlockSpec((COLS, LANES), lambda i: (i, 0)),
        ),
        compiler_params=pltpu.CompilerParams(vmem_limit_bytes=VMEM_LIMIT),
        cost_estimate=pl.CostEstimate(
            flops=4 * tokens * COLS * heads * HS,
            bytes_accessed=2 * tokens * width + 4 * tokens * heads * HS,
            transcendentals=tokens * COLS * heads,
        ),
    )(qkv)


def column_kernel(qkv_ref, mean_ref, stat_ref, *, heads):
    lines = qkv_ref.shape[0]
    count = lines * GROUP
    line = lax.broadcasted_iota(jnp.int32, (count, count), 0)
    lane = lax.broadcasted_iota(jnp.int32, (count, count), 1)
    allowed = jnp.logical_and(
        lax.rem(line, GROUP) == lax.rem(lane, GROUP), line // GROUP > lane // GROUP
    )
    place = lax.broadcasted_iota(jnp.int32, (count, LANES), 1)
    some = lax.broadcasted_iota(jnp.int32, (count, 1), 0) >= GROUP
    stats = jnp.zeros((count, LANES), F32)
    for head in range(heads):
        at = head * 3 * HS
        queries, keys, values = (
            qkv_ref[:, :, at + i * HS : at + (i + 1) * HS].reshape(count, HS) for i in range(3)
        )
        _, top, weights, factor = softmax_part(queries, keys, None, allowed)
        weights = jnp.where(allowed, weights, 0.0)
        total = jnp.sum(weights, axis=1, keepdims=True)
        summed = jnp.dot(weights.astype(BF16), values, preferred_element_type=F32)
        mean = jnp.where(some, summed / jnp.where(some, total, 1.0), 0.0)
        mean_ref[:, :, head * HS : (head + 1) * HS] = mean.astype(BF16).reshape(
            lines, GROUP, HS
        )
        stats = jnp.where(place == head, jnp.where(some, top * factor, NEGATIVE), stats)
        stats = jnp.where(place == heads + head, total, stats)
    stat_ref[0] = stats.T[: stat_ref.shape[1], :]


def column_attention(qkv, heads, held):
    lines, columns, width = qkv.shape
    groups = columns // GROUP
    return pl.pallas_call(
        functools.partial(column_kernel, heads=heads),
        out_shape=(
            jax.ShapeDtypeStruct((lines, columns, heads * HS), BF16),
            jax.ShapeDtypeStruct((groups, held, lines * GROUP), F32),
        ),
        grid=(groups,),
        in_specs=[pl.BlockSpec((lines, GROUP, width), lambda i: (0, i, 0))],
        out_specs=(
            pl.BlockSpec((lines, GROUP, heads * HS), lambda i: (0, i, 0)),
            pl.BlockSpec((1, held, lines * GROUP), lambda i: (i, 0, 0)),
        ),
        compiler_params=pltpu.CompilerParams(vmem_limit_bytes=VMEM_LIMIT),
    )(qkv)


def merge_kernel(acc_ref, rstat_ref, mean_ref, cstat_ref, out_ref, *, heads):
    rstat = rstat_ref[...]
    held, block = cstat_ref.shape[1:]
    cstat = cstat_ref[0]
    if held < LANES:
        cstat = jnp.concatenate([cstat, jnp.zeros((LANES - held, block), F32)], axis=0)
    cstat = cstat.T
    sources, _, columns, _ = mean_ref.shape
    for head in range(heads):
        across = slice(head * HS, (head + 1) * HS)
        row_max = rstat[:, head : head + 1]
        row_total = rstat[:, heads + head : heads + head + 1]
        col_max = cstat[:, head : head + 1]
        col_total = cstat[:, heads + head : heads + head + 1]
        top = jnp.maximum(row_max, col_max)
        row_factor = jnp.exp(row_max - top)
        col_part = jnp.exp(col_max - top) * col_total
        share = 1.0 / (row_factor * row_total + col_part)
        mean = mean_ref[:, 0, :, across].reshape(sources * columns, HS).astype(F32)
        out_ref[:, across] = (
            (row_factor * share) * acc_ref[:, across] + (col_part * share) * mean
        ).astype(BF16)


def remote(src, dst, sems, at, target):
    return pltpu.make_async_remote_copy(
        src_ref=src,
        dst_ref=dst,
        send_sem=sems[0].at[at],
        recv_sem=sems[1].at[at],
        device_id=target,
        device_id_type=pl.DeviceIdType.MESH,
    )


def ring_place(row, half):
    return (row // 2) * (1 - row % 2) + (2 * half - 1 - row // 2) * (row % 2)


def ring_row(place, half):
    over = place // half
    return 2 * place * (1 - over) + (2 * (2 * half - 1 - place) + 1) * over


def arrive_kernel(
    signal_ref,
    weight_ref,
    crossed_ref,
    whole_ref,
    cross_send,
    cross_recv,
    peer_send,
    peer_recv,
    twin_send,
    twin_recv,
    ring_send,
    ring_recv,
    local_sem,
    *,
    count,
    pieces,
):
    row, col = lax.axis_index("row"), lax.axis_index("col")
    rows_here = signal_ref.shape[0]
    depth = weight_ref.shape[0]
    half = count // 2
    chips = pieces // 2
    twin = (row, col + 1 - 2 * (col % 2))
    peers = [(row, (col + 2 * k) % pieces) for k in range(1, chips)]
    others = [((row + k) % count, col) for k in range(1, count)]

    barrier = pltpu.get_barrier_semaphore()
    for target in others + peers + [twin]:
        pl.semaphore_signal(
            barrier, inc=1, device_id=target, device_id_type=pl.DeviceIdType.MESH
        )
    pl.semaphore_wait(barrier, len(others) + len(peers) + 1)

    def chunk(source_row, source_col):
        return crossed_ref.at[source_col, pl.ds(source_row * rows_here, rows_here)]

    started = []

    def go(copy):
        copy.start()
        started.append(copy)
        return copy

    own = signal_ref.at[:, row]
    keep = pltpu.make_async_copy(own, chunk(row, col), local_sem.at[0])
    keep.start()
    place = ring_place(row, half)
    after = (ring_row((place + 1) % count, half), col)
    before = (ring_row((place + count - 1) % count, half), col)

    def shard(owner, step):
        if step < half - 1:
            return [pl.ds(owner * depth, depth)] * 2
        return [
            pl.ds(owner * depth, depth // 2),
            pl.ds(owner * depth + depth // 2, depth // 2),
        ]

    ring = []

    def ring_step(step):
        for way, target in ((0, after), (1, before)):
            offset = count - step if way == 0 else step
            owner = ring_row((place + offset) % count, half)
            where = shard(owner, step)[way]
            if step == 0:
                source = weight_ref
                if half == 1:
                    source = weight_ref.at[pl.ds(way * (depth // 2), depth // 2)]
            else:
                source = whole_ref.at[where]
            ring.append(
                go(
                    remote(
                        source,
                        whole_ref.at[where],
                        (ring_send, ring_recv),
                        2 * step + way,
                        target,
                    )
                )
            )

    def spread(at, source, source_row):
        sent = []
        for j, target in enumerate(peers):
            sent.append(
                go(
                    remote(
                        source,
                        chunk(source_row, col),
                        (peer_send, peer_recv),
                        at * (chips - 1) + j,
                        target,
                    )
                )
            )
        go(remote(source, chunk(source_row, col), (twin_send, twin_recv), at * chips, twin))
        return sent

    def pass_on(at, sent, source_row):
        for j, copy in enumerate(sent):
            copy.wait_recv()
            piece = chunk(source_row, (col + pieces - 2 * (j + 1)) % pieces)
            go(remote(piece, piece, (twin_send, twin_recv), at * chips + 1 + j, twin))

    crossing = []
    for k, target in enumerate(others):
        crossing.append(
            go(
                remote(
                    signal_ref.at[:, target[0]],
                    chunk(row, col),
                    (cross_send, cross_recv),
                    k,
                    target,
                )
            )
        )
    pending = (0, spread(0, own, row), row)
    ring_step(0)
    hold = pltpu.make_async_copy(
        weight_ref, whole_ref.at[pl.ds(row * depth, depth)], local_sem.at[1]
    )
    hold.start()
    step = 1
    for k in range(1, count):
        crossing[k - 1].wait_recv()
        source_row = (row + count - k) % count
        later = (k, spread(k, chunk(source_row, col), source_row), source_row)
        pass_on(*pending)
        pending = later
        if k % 2 == 0 and step < half:
            for copy in ring[2 * step - 2 : 2 * step]:
                copy.wait_recv()
            ring_step(step)
            step += 1
    pass_on(*pending)
    for copy in ring[2 * half - 2 :]:
        copy.wait_recv()
    for at in range(count * chips):
        remote(own, chunk(row, col), (twin_send, twin_recv), at, twin).wait_recv()
    for copy in started:
        copy.wait_send()
    keep.wait()
    hold.wait()


def arrive(signal, weight, count, pieces):
    rows_here, _, columns, width = signal.shape
    depth, outs = weight.shape
    chips = pieces // 2
    dma = pltpu.SemaphoreType.DMA
    sizes = (count - 1, max(1, count * (chips - 1)), count * chips, count)
    return pl.pallas_call(
        functools.partial(arrive_kernel, count=count, pieces=pieces),
        out_shape=(
            jax.ShapeDtypeStruct((pieces, rows_here * count, columns, width), BF16),
            jax.ShapeDtypeStruct((depth * count, outs), BF16),
        ),
        in_specs=[pl.BlockSpec(memory_space=pl.ANY)] * 2,
        out_specs=(pl.BlockSpec(memory_space=pl.ANY),) * 2,
        scratch_shapes=[dma((size,)) for size in sizes for _ in range(2)] + [dma((2,))],
        compiler_params=pltpu.CompilerParams(collective_id=0, has_side_effects=True),
        cost_estimate=pl.CostEstimate(
            flops=0, bytes_accessed=300 * 1024 * 1024, transcendentals=0
        ),
    )(signal, weight)


def finish_kernel(
    acc_ref,
    rstat_ref,
    mean_ref,
    cstat_ref,
    weight_ref,
    signal_ref,
    out_ref,
    held_ref,
    peer_send,
    peer_recv,
    twin_send,
    twin_recv,
    *,
    heads,
    block,
):
    row, col = lax.axis_index("row"), lax.axis_index("col")
    pieces, tokens, _ = held_ref.shape
    chips = pieces // 2
    twin = (row, col + 1 - 2 * (col % 2))
    peers = [(row, (col + 2 * k) % pieces) for k in range(1, chips)]
    barrier = pltpu.get_barrier_semaphore()
    for target in peers + [twin]:
        pl.semaphore_signal(
            barrier, inc=1, device_id=target, device_id_type=pl.DeviceIdType.MESH
        )
    pl.semaphore_wait(barrier, len(peers) + 1)

    started = []

    def send(at, owner, sems, index, target):
        piece = held_ref.at[owner, pl.ds(at * block, block)]
        copy = remote(piece, piece, sems, index, target)
        copy.start()
        started.append(copy)
        return copy

    arriving, passed = [], []
    for line in range(tokens // COLS):
        rows = pl.ds(line * COLS, COLS)
        merge_kernel(
            acc_ref.at[rows],
            rstat_ref.at[rows],
            mean_ref.at[:, pl.ds(line, 1)],
            cstat_ref.at[pl.ds(line, 1)],
            held_ref.at[col, rows],
            heads=heads,
        )
        for at in range(line * COLS // block, (line + 1) * COLS // block):
            arriving.append(
                [
                    send(at, col, (peer_send, peer_recv), at * (chips - 1) + j, target)
                    for j, target in enumerate(peers)
                ]
            )
            passed.append([send(at, col, (twin_send, twin_recv), at * chips, twin)])

    def multiply(at):
        for copy in passed[at]:
            copy.wait_recv()
        rows = pl.ds(at * block, block)
        joined = jnp.concatenate([held_ref[i, rows, :] for i in range(pieces)], axis=1)
        branch = jnp.dot(joined, weight_ref[...], preferred_element_type=F32)
        out_ref[rows, :] = (signal_ref[rows, :].astype(F32) + branch).astype(BF16)

    for at in range(tokens // block):
        for j, copy in enumerate(arriving[at]):
            copy.wait_recv()
            owner = (col + pieces - 2 * (j + 1)) % pieces
            passed[at].append(
                send(at, owner, (twin_send, twin_recv), at * chips + 1 + j, twin)
            )
        if at > 0:
            multiply(at - 1)
    multiply(tokens // block - 1)
    for copy in started:
        copy.wait_send()


def finish(row_acc, row_stats, col_mean, col_stats, weight, signal, heads, pieces):
    tokens, width = row_acc.shape
    outs = weight.shape[1]
    block = block_of(COLS, 256)
    chips = pieces // 2
    chunks = tokens // block
    dma = pltpu.SemaphoreType.DMA
    sizes = (max(1, chunks * (chips - 1)), chunks * chips)
    return pl.pallas_call(
        functools.partial(finish_kernel, heads=heads, block=block),
        out_shape=jax.ShapeDtypeStruct((tokens, outs), BF16),
        in_specs=[pl.BlockSpec(memory_space=pltpu.VMEM)] * 6,
        out_specs=pl.BlockSpec(memory_space=pltpu.VMEM),
        scratch_shapes=[pltpu.VMEM((pieces, tokens, width), BF16)]
        + [dma((size,)) for size in sizes for _ in range(2)],
        compiler_params=pltpu.CompilerParams(
            collective_id=1, has_side_effects=True, vmem_limit_bytes=VMEM_LIMIT
        ),
        cost_estimate=pl.CostEstimate(
            flops=2 * tokens * pieces * width * outs,
            bytes_accessed=150 * 1024 * 1024,
            transcendentals=0,
        ),
    )(row_acc, row_stats, col_mean, col_stats, weight, signal)


def per_device(signal, norm_gain, qkv_weight, out_weight):
    samples, width = signal.shape
    count = lax.axis_size("row")
    rows_here = samples // COLS
    lines = rows_here * count
    columns = COLS // count
    heads = qkv_weight.shape[1] // (3 * HS)
    held = -(-2 * heads // 8) * 8

    pieces = lax.axis_size("col")
    col_signal, piece_qkv = arrive(
        signal.reshape(rows_here, count, columns, width), qkv_weight, count, pieces
    )
    col_signal = col_signal.reshape(pieces, lines * columns, width)
    row_signal = lax.all_gather(signal, "col", axis=0)
    piece_out = lax.all_gather(out_weight, "row", axis=0, tiled=True)

    col_qkv = norm_project(col_signal, norm_gain, piece_qkv)
    col_mean, col_stats = column_attention(
        col_qkv.reshape(lines, columns, 3 * heads * HS), heads, held
    )
    col_stats = jnp.transpose(
        col_stats.reshape(columns // GROUP, held, lines, GROUP), (2, 1, 0, 3)
    ).reshape(lines, held, columns)
    col_stats = lax.all_to_all(col_stats, "row", split_axis=0, concat_axis=2, tiled=True)
    col_mean = lax.all_to_all(
        col_mean.reshape(count, rows_here, columns, heads * HS),
        "row",
        split_axis=0,
        concat_axis=0,
        tiled=True,
    )
    row_qkv = norm_project(row_signal, norm_gain, piece_qkv)
    row_acc, row_stats = row_attention(row_qkv, heads)
    return finish(
        row_acc, row_stats, col_mean, col_stats, piece_out, signal, heads, pieces
    )


def solution(mesh):
    return jax.shard_map(
        per_device,
        mesh=mesh,
        in_specs=(P("row", "col"), P(), P("row", "col"), P("row", "col")),
        out_specs=P("row", "col"),
        check_vma=False,
    )
```
